512 devices in a mesh: row: 16 (over y, x), col: 16 (over z), dep: 2 (over core).
Axes of the slice: x: 4, y: 4, z: 16, core: 2. Of those that a mesh axis runs over, the one named last changes fastest.
Arguments:
- features: bfloat16 [32768, 256], P(('col', 'row')), may hold values from -6 to 6
- weight: bfloat16 [256, 256], P(None, 'dep'), may hold values from -0.375 to 0.375
- tiles: bfloat16 [16, 16, 128, 128, 128], P('row', 'col'), may hold values from -0.1875 to 0.1875
- tile_blocks: int32 [16, 16, 2, 128], P('row', 'col'), may hold values from 0 to 15, as said below
- tile_counts: int32 [16, 16], P('row', 'col'), may hold values from 16 to 128, as said below
- cotangent: bfloat16 [32768, 256], P(('row', 'col'), 'dep'), may hold values from -6 to 6
Outputs:
- activations: bfloat16 [32768, 256], P(('row', 'col'), 'dep')
- feature_grad: bfloat16 [32768, 256], P(('col', 'row'), 'dep')
- weight_grad: float32 [256, 256], P(None, 'dep')
The draws below stay inside these ranges and needn't reach their ends.
Inputs may be any that keep to these rules, and one draw needn't show every extreme that they name: `tile_blocks`: live slots of one grid position name distinct block pairs; padding slots also hold valid block numbers. `tile_counts`: each count is 128 divided by 1, 2, 4 or 8; at least one grid position holds exactly 128 live slots.
All inputs are finite; a program needn't handle non-finite values.
Results may differ from the reference program's by a relative error of at most 0.034.
Values may be sent and summed in bfloat16 or wider, within the bound.
A program may use at most 64 MiB of HBM per device.

```python
import jax
import jax.numpy as jnp
from jax import lax

F = 256
BLOCK = 128
BPP = 16
TMAX = 128
NODES = 32768
N_ROW = 16
N_COL = 16


def draw_tile_blocks(key, part):
    key = jax.random.fold_in(key, 23)
    keys = jax.random.split(key, N_ROW * N_COL)
    orders = jax.vmap(lambda single: jax.random.permutation(single, BPP * BPP))(keys)
    chosen = orders[:, :TMAX].astype(jnp.int32)
    block_rows = chosen // BPP
    block_column_count = chosen % BPP
    stacked = jnp.stack([block_rows, block_column_count], axis=1)
    return stacked.reshape(N_ROW, N_COL, 2, TMAX).astype(jnp.int32)


def draw_tile_counts(key, part):
    key = jax.random.fold_in(key, 11)
    first, second = jax.random.split(key)
    grid_levels = jax.random.randint(first, (N_ROW * N_COL,), 0, 4)
    full_at = jax.random.randint(second, (), 0, N_ROW * N_COL)
    grid_levels = jnp.where(jnp.arange(N_ROW * N_COL) == full_at, 0, grid_levels)
    divisors = jnp.array([1, 2, 4, 8], jnp.int32)[grid_levels]
    return (TMAX // divisors).reshape(N_ROW, N_COL).astype(jnp.int32)


def shard_levels(rng, dims, cuts, low, high):
    gain, own = 1.0, jax.random.fold_in(rng, 6)
    for position, parts in cuts:
        draws = jnp.exp(jax.random.uniform(jax.random.fold_in(own, position), (parts,), jnp.float32, low / len(cuts), high / len(cuts)))
        gain = gain * jnp.repeat(draws, dims[position] // parts).reshape([-1 if axis == position else 1 for axis in range(len(dims))])
    return gain


def gaussian(own_key, dims, scale, bound, cuts=(), kind=jnp.bfloat16):
    result = jax.random.normal(own_key, dims, jnp.float32) * scale
    if len(cuts) > 0:
        result = shard_levels(own_key, dims, cuts, -0.22, 0.18) * result
    return jnp.clip(result, min=-bound, max=bound).astype(kind)


def setup_inputs(seed: int = 0) -> dict:
    splits = jax.random.split(jax.random.key(seed), 7)
    return {
        "features": gaussian(splits[0], (NODES, F), 1.0, 6.0, ((0, 256),)),
        "weight": gaussian(splits[1], (F, F), F ** -0.5, 0.375, ((1, 2),)),
        "tiles": gaussian(splits[2], (N_ROW, N_COL, TMAX, BLOCK, BLOCK), (BLOCK * TMAX // BPP) ** -0.5, 0.1875, ((0, 16), (1, 16))),
        "tile_blocks": draw_tile_blocks(jax.random.fold_in(splits[6], 71), 0),
        "tile_counts": draw_tile_counts(jax.random.fold_in(splits[6], 71), 0),
        "cotangent": gaussian(splits[5], (NODES, F), 1.0, 6.0, ((0, 256), (1, 2))),
    }


def reference(features, weight, tiles, tile_blocks, tile_counts, cotangent):
    projected = jnp.dot(features, weight, preferred_element_type=jnp.float32).astype(jnp.bfloat16)
    proj_blocks = projected.reshape(N_COL, BPP, BLOCK, F)
    slot_ids = jnp.arange(TMAX, dtype=jnp.int32)
    positions = jnp.arange(N_ROW * N_COL, dtype=jnp.int32)

    def forward_step(carry, index):
        row_at = index // N_COL
        col_at = index % N_COL
        tile_set = tiles[row_at, col_at].astype(jnp.float32)
        blocks = tile_blocks[row_at, col_at]
        live = (slot_ids < tile_counts[row_at, col_at]).astype(jnp.float32)
        source = proj_blocks[col_at][blocks[1]].astype(jnp.float32)
        product = jnp.einsum("tab,tbf->taf", tile_set, source) * live[:, None, None]
        part = jax.ops.segment_sum(product, blocks[0], num_segments=BPP)
        return carry.at[row_at].add(part), None

    start = jnp.zeros((N_ROW, BPP, BLOCK, F), jnp.float32)
    pre, _ = lax.scan(forward_step, start, positions)
    pre = pre.reshape(NODES, F)
    squash = jnp.tanh(pre)
    activations = squash.astype(jnp.bfloat16)
    slope = (cotangent.astype(jnp.float32) * (1.0 - squash * squash)).astype(jnp.bfloat16)
    slope_blocks = slope.reshape(N_ROW, BPP, BLOCK, F)

    def backward_step(carry, index):
        row_at = index // N_COL
        col_at = index % N_COL
        tile_set = tiles[row_at, col_at].astype(jnp.float32)
        blocks = tile_blocks[row_at, col_at]
        live = (slot_ids < tile_counts[row_at, col_at]).astype(jnp.float32)
        source = slope_blocks[row_at][blocks[0]].astype(jnp.float32)
        product = jnp.einsum("tab,taf->tbf", tile_set, source) * live[:, None, None]
        part = jax.ops.segment_sum(product, blocks[1], num_segments=BPP)
        return carry.at[col_at].add(part), None

    start_back = jnp.zeros((N_COL, BPP, BLOCK, F), jnp.float32)
    spread, _ = lax.scan(backward_step, start_back, positions)
    spread_half_width = spread.reshape(NODES, F).astype(jnp.bfloat16)
    feature_grad = jnp.dot(spread_half_width, weight.T, preferred_element_type=jnp.float32).astype(jnp.bfloat16)
    weight_grad = jnp.dot(features.T, spread_half_width, preferred_element_type=jnp.float32)
    return activations, feature_grad, weight_grad
```

```python
import functools

import jax
import jax.numpy as jnp
from jax import lax
from jax.experimental import pallas as pl
from jax.experimental.pallas import tpu as pltpu
from jax.sharding import PartitionSpec as P

MESH = pl.DeviceIdType.MESH
F32, BF16 = jnp.float32, jnp.bfloat16
B = 128
BPP = 16
NODES = BPP * B
HB = B // 2
NX, NY, NZ = 4, 4, 16
XY = sorted(
    [(dx, dy) for dx in (0, 1, -1, 2) for dy in (0, 1, -1, 2) if (dx, dy) != (0, 0)],
    key=lambda o: -(abs(o[0]) + abs(o[1])),
)
FIRST = (6, -6, 3, -3, 1, -1)
CHILDREN = {6: (8, 7, 5), -6: (-7, -5), 3: (4, 2), -3: (-4, -2), 1: (), -1: ()}
LEAVES = (8, 7, -7, 5, -5, 4, -4, 2, -2)
PARENT = {d: p for p, ds in CHILDREN.items() for d in ds}
PEERS = (
    [(dx, dy, 0, 0) for dx, dy in XY]
    + [(0, 0, d, 0) for d in range(1, NZ)]
    + [(0, 0, d, 1) for d in FIRST]
    + [(0, 0, 0, 1)]
)
N_SEMS = 15 + 9 + 13 + 3 + 13 + 9 + 15 + 1 + 15 + 15 + 15


def kernel(
    feat, weight, cot, blocks, counts, tiles, act_out, fg_out, wg_out,
    tile_v, dense, gath, inv_v, inv_s, w_all, cot_h, leaf_s, leaf_r, part, first_s, first_r, sib_s, sib_r, agg,
    act_s, act_r, slope_s, slope_p, spread_t, back_s, back_r, wgp, wg_s, wg_r, wg_t, wc_s, wc_r, wz, wt,
    tile_sem, inv_sem, send_sem, recv_sem,
):
    i = lax.axis_index("row")
    z = lax.axis_index("col")
    c = lax.axis_index("dep")
    x, y = lax.rem(i, NX), lax.div(i, NX)

    def row_at(dx, dy):
        return lax.rem(y + (dy + NY), NY) * NX + lax.rem(x + (dx + NX), NX)

    def z_at(d):
        return lax.rem(z + (d + NZ), NZ)

    def device(dx, dy, dz, dc):
        return (row_at(dx, dy), z_at(dz), 1 - c if dc else c)

    def block(at, size=B):
        return pl.ds(pl.multiple_of(at * size, size), size)

    counter = [0]
    sent = []

    def send(src, dst, where):
        k = counter[0]
        counter[0] += 1
        copy = pltpu.make_async_remote_copy(
            src_ref=src, dst_ref=dst, send_sem=send_sem.at[k], recv_sem=recv_sem.at[k],
            device_id=where, device_id_type=MESH,
        )
        copy.start()
        sent.append(copy)
        return copy

    def send_both(srcs, dst, landed, z_to):
        k = counter[0]
        counter[0] += 2
        copies = [
            pltpu.make_async_remote_copy(
                src_ref=srcs[q], dst_ref=dst, send_sem=send_sem.at[k + q], recv_sem=recv_sem.at[k + c],
                device_id=(i, z_to, jnp.int32(q)), device_id_type=MESH,
            )
            for q in range(2)
        ]
        for copy in copies:
            copy.start()
        sent.extend(copies)
        return [
            pltpu.make_async_remote_copy(
                src_ref=srcs[q], dst_ref=landed(q), send_sem=send_sem.at[k + q], recv_sem=recv_sem.at[k + q],
                device_id=(i, z_to, jnp.int32(q)), device_id_type=MESH,
            )
            for q in range(2)
        ]

    loads = []
    for q in range(4):
        load = pltpu.make_async_copy(
            tiles.at[0, 0, pl.ds(q * 32, 32)], tile_v.at[pl.ds(q * 32, 32)], tile_sem.at[q]
        )
        load.start()
        loads.append(load)
    barrier = pltpu.get_barrier_semaphore()
    for peer in PEERS:
        pl.semaphore_signal(barrier, inc=1, device_id=device(*peer), device_id_type=MESH)

    flat = blocks[0, 0, 0:1, :] * BPP + blocks[0, 0, 1:2, :]
    lane = lax.broadcasted_iota(jnp.int32, (1, B), 1)
    flat = jnp.where(lane < counts[0, 0], flat, -1)
    flat = jnp.broadcast_to(flat, (B, B)).T
    slot = lax.broadcasted_iota(jnp.int32, (B, B), 0) - B
    place = lax.broadcasted_iota(jnp.int32, (B, B), 1)
    inv_v[...] = jnp.zeros_like(inv_v)
    for h in range(2):
        hit = jnp.where(flat == place + h * B, slot, 0)
        inv_v[h : h + 1, :] = jnp.clip(jnp.sum(hit, axis=0, keepdims=True) + B, 0, B)
    inv_copy = pltpu.make_async_copy(inv_v, inv_s, inv_sem)
    inv_copy.start()
    tile_v[B] = jnp.zeros((B, B), BF16)

    own = block(i)
    gath[own, :] = feat[:, block(c)]
    w_all[c] = weight[...]
    cot_h[c] = cot[block(c, HB), :]

    pl.semaphore_wait(barrier, len(PEERS))

    gathered = [send(gath.at[own], gath.at[own], device(dx, dy, 0, 0)) for dx, dy in XY]
    got_w = send(weight, w_all.at[c], device(0, 0, 0, 1))
    got_cot = send(cot.at[block(1 - c, HB)], cot_h.at[c], device(0, 0, 0, 1))

    inv_copy.wait()
    for load in loads:
        load.wait()

    @pl.loop(0, BPP)
    def _(r):
        rows = block(r)
        for col in range(BPP):
            at = r * BPP + col
            dense[rows, col * B : (col + 1) * B] = tile_v[inv_s[lax.div(at, B), lax.rem(at, B)]]

    for copy in gathered:
        copy.wait_recv()

    def chunk(d):
        return jnp.dot(dense[block(z_at(-d)), :], gath[...], preferred_element_type=F32)

    leaf_copy = {}
    for k, d in enumerate(LEAVES):
        leaf_s[k] = chunk(d).astype(BF16)
        leaf_copy[d] = send(leaf_s.at[k], leaf_r.at[k], device(0, 0, PARENT[d] - d, 0))

    def send_first(k, p, value):
        first_s[k] = value.astype(BF16)
        halves = [first_s.at[k, pl.ds(q * HB, HB)] for q in range(2)]
        return send_both(halves, first_r.at[k, c], lambda q: first_r.at[k, q], z_at(-p))

    first_copy = {}
    for k, p in enumerate(FIRST):
        if CHILDREN[p]:
            part[k] = chunk(p)
    for k, p in enumerate(FIRST):
        if not CHILDREN[p]:
            first_copy[p] = send_first(k, p, chunk(p))
    mine = chunk(0)
    part[len(FIRST)] = mine
    sib_s[...] = part[len(FIRST), block(1 - c, HB), :].astype(BF16)
    sib_copy = send(sib_s, sib_r, device(0, 0, 0, 1))
    for p in (3, -3, 6, -6):
        k = FIRST.index(p)
        total = part[k]
        for d in CHILDREN[p]:
            leaf_copy[d].wait_recv()
            total = total + leaf_r[LEAVES.index(d)].astype(F32)
        first_copy[p] = send_first(k, p, total)
    agg[c] = part[len(FIRST), block(c, HB), :]
    sib_copy.wait_recv()
    agg[1 - c] = sib_r[...].astype(F32)
    got_w.wait_recv()
    got_cot.wait_recv()
    for p in (1, -1, 3, -3, 6, -6):
        for copy in first_copy[p]:
            copy.wait_recv()
    halves = []
    for h in range(2):
        total = agg[h]
        for k in range(len(FIRST)):
            total = total + first_r[k, h].astype(F32)
        halves.append(total.astype(BF16))

    slopes = []
    for u in range(2):
        pre = sum(
            jnp.dot(halves[h], w_all[u, h * B : (h + 1) * B, :], preferred_element_type=F32) for h in range(2)
        )
        squash = jnp.tanh(pre)
        act_s[u] = squash.astype(BF16)
        slopes.append((cot_h[u].astype(F32) * (1.0 - squash * squash)).astype(BF16))
    for h in range(2):
        back = sum(
            lax.dot_general(
                slopes[u], w_all[u, h * B : (h + 1) * B, :], (((1,), (1,)), ((), ())), preferred_element_type=F32
            )
            for u in range(2)
        )
        slope_s[h] = back.astype(BF16)

    here = pl.ds(pl.multiple_of(z * B + c * HB, HB), HB)
    out_copy = {}
    for p in FIRST:

        def landed(q, p=p):
            return slope_p.at[pl.ds(pl.multiple_of(z_at(-p) * B + q * HB, HB), HB)]

        out_copy[p] = send_both([slope_s.at[q] for q in range(2)], slope_p.at[here], landed, z_at(p))
    near = send(slope_s.at[1 - c], slope_p.at[here], device(0, 0, 0, 1))
    slope_p[here, :] = slope_s[c]
    act_copy = send(act_s.at[1 - c], act_r, device(0, 0, 0, 1))
    act_out[block(c, HB), :] = act_s[c]

    for u in range(2):
        for h in range(2):
            wgp[u, h * B : (h + 1) * B, :] = lax.dot_general(
                halves[h], slopes[u], (((0,), (0,)), ((), ())), preferred_element_type=F32
            )
    wg_s[...] = wgp[1 - c].astype(BF16)
    wg_copy = send(wg_s, wg_r, device(0, 0, 0, 1))

    leaf_out = {}
    for p in (3, -3, 6, -6):
        for copy in out_copy[p]:
            copy.wait_recv()
        rows = block(z_at(-p))
        for d in CHILDREN[p]:
            leaf_out[d] = send(slope_p.at[rows], slope_p.at[rows], device(0, 0, d - p, 0))

    wg_copy.wait_recv()
    wg_t[...] = wgp[c] + wg_r[...].astype(F32)
    wc_s[...] = wg_t[...].astype(BF16)
    wc_copy = [
        send(wc_s.at[block(row_at(dx, dy), 16)], wc_r.at[k], device(dx, dy, 0, 0))
        for k, (dx, dy) in enumerate(XY)
    ]

    near.wait_recv()
    for p in (1, -1):
        for copy in out_copy[p]:
            copy.wait_recv()
    act_copy.wait_recv()
    act_out[block(1 - c, HB), :] = act_r[...]
    for copy in wc_copy:
        copy.wait_recv()
    total = wg_t[block(i, 16), :]
    for k in range(len(XY)):
        total = total + wc_r[k].astype(F32)
    wz[z] = total.astype(BF16)
    wz_copy = [send(wz.at[z], wz.at[z], device(0, 0, d, 0)) for d in range(1, NZ)]

    for d in LEAVES:
        leaf_out[d].wait_recv()

    @pl.loop(0, 4)
    def _(q):
        cols = block(q, 512)
        value = lax.dot_general(
            slope_p[...], dense[:, cols], (((0,), (0,)), ((), ())), preferred_element_type=F32
        )
        for k in range(4):
            spread_t[q * 4 + k] = value[:, k * B : (k + 1) * B]
            back_s[q * 4 + k] = value[:, k * B : (k + 1) * B].astype(BF16)

    back_copy = [
        send(back_s.at[row_at(dx, dy)], back_r.at[k], device(dx, dy, 0, 0)) for k, (dx, dy) in enumerate(XY)
    ]

    for copy in wz_copy:
        copy.wait_recv()
    total = wz[0].astype(F32)
    for k in range(1, NZ):
        total = total + wz[k].astype(F32)
    wt[block(i, 16), :] = total
    wt_copy = [
        send(wt.at[block(i, 16)], wt.at[block(i, 16)], device(dx, dy, 0, 0)) for dx, dy in XY
    ]

    for copy in back_copy:
        copy.wait_recv()
    total = spread_t[i]
    for k in range(len(XY)):
        total = total + back_r[k].astype(F32)
    fg_out[...] = total.T.astype(BF16)

    for copy in wt_copy:
        copy.wait_recv()
    wg_out[...] = wt[...]
    for copy in sent:
        copy.wait_send()


def per_device(features, weight, tiles, tile_blocks, tile_counts, cotangent):
    vmem = pl.BlockSpec(memory_space=pltpu.VMEM)
    smem = pl.BlockSpec(memory_space=pltpu.SMEM)
    n_xy = len(XY)
    scratch = [
        pltpu.VMEM((B + 1, B, B), BF16),
        pltpu.VMEM((NODES, NODES), BF16),
        pltpu.VMEM((NODES, B), BF16),
        pltpu.VMEM((8, B), jnp.int32),
        pltpu.SMEM((8, B), jnp.int32),
        pltpu.VMEM((2, 2 * B, B), BF16),
        pltpu.VMEM((2, HB, B), BF16),
        pltpu.VMEM((9, B, B), BF16),
        pltpu.VMEM((9, B, B), BF16),
        pltpu.VMEM((7, B, B), F32),
        pltpu.VMEM((6, B, B), BF16),
        pltpu.VMEM((6, 2, HB, B), BF16),
        pltpu.VMEM((HB, B), BF16),
        pltpu.VMEM((HB, B), BF16),
        pltpu.VMEM((2, HB, B), F32),
        pltpu.VMEM((2, HB, B), BF16),
        pltpu.VMEM((HB, B), BF16),
        pltpu.VMEM((2, HB, B), BF16),
        pltpu.VMEM((NODES, B), BF16),
        pltpu.VMEM((BPP, B, B), F32),
        pltpu.VMEM((BPP, B, B), BF16),
        pltpu.VMEM((n_xy, B, B), BF16),
        pltpu.VMEM((2, 2 * B, B), F32),
        pltpu.VMEM((2 * B, B), BF16),
        pltpu.VMEM((2 * B, B), BF16),
        pltpu.VMEM((2 * B, B), F32),
        pltpu.VMEM((2 * B, B), BF16),
        pltpu.VMEM((n_xy, 16, B), BF16),
        pltpu.VMEM((NZ, 16, B), BF16),
        pltpu.VMEM((2 * B, B), F32),
        pltpu.SemaphoreType.DMA((4,)),
        pltpu.SemaphoreType.DMA,
        pltpu.SemaphoreType.DMA((N_SEMS,)),
        pltpu.SemaphoreType.DMA((N_SEMS,)),
    ]
    return tuple(
        pl.pallas_call(
            kernel,
            out_shape=(
                jax.ShapeDtypeStruct((B, B), BF16),
                jax.ShapeDtypeStruct((B, B), BF16),
                jax.ShapeDtypeStruct((2 * B, B), F32),
            ),
            in_specs=[vmem, vmem, vmem, vmem, smem, pl.BlockSpec(memory_space=pl.ANY)],
            out_specs=(vmem, vmem, vmem),
            scratch_shapes=scratch,
            compiler_params=pltpu.CompilerParams(
                collective_id=0, has_side_effects=True, vmem_limit_bytes=56 * 2**20
            ),
            cost_estimate=pl.CostEstimate(flops=4 * NODES * NODES * B, bytes_accessed=2**23, transcendentals=B * B),
            name="gcn",
        )(features, weight, cotangent, tile_blocks, tile_counts, tiles)
    )


def solution(mesh):
    return jax.shard_map(
        per_device,
        mesh=mesh,
        in_specs=(
            P(("col", "row"), None),
            P(None, "dep"),
            P("row", "col", None, None, None),
            P("row", "col", None, None),
            P("row", "col"),
            P(("row", "col"), "dep"),
        ),
        out_specs=(P(("row", "col"), "dep"), P(("col", "row"), "dep"), P(None, "dep")),
        check_vma=False,
    )
```

```python
import functools

import jax
import jax.numpy as jnp
from jax import lax
from jax.experimental import pallas as pl
from jax.experimental.pallas import tpu as pltpu
from jax.sharding import PartitionSpec as P

MESH = pl.DeviceIdType.MESH
F32, BF16 = jnp.float32, jnp.bfloat16
B = 128
BPP = 16
NODES = BPP * B
HB = B // 2
NX, NY, NZ = 4, 4, 16
XY = sorted(
    [(dx, dy) for dx in (0, 1, -1, 2) for dy in (0, 1, -1, 2) if (dx, dy) != (0, 0)],
    key=lambda o: -(abs(o[0]) + abs(o[1])),
)
FIRST = (5, -5, 2, -2, 1, -1)
INNER = (5, -5, 2, -2)
LEAVES = (8, 7, -7, 6, -6, 4, -4, 3, -3)
CHILDREN = {5: (7, 6, 4), -5: (-7, -6, -4), 2: (3,), -2: (-3,), 1: (), -1: ()}
PARENT = {d: p for p, ds in CHILDREN.items() for d in ds}


def children(p, h):
    pairs = [(d, d - p) for d in CHILDREN[p]]
    if p == 5 and h == 0:
        pairs = [(8, 3)] + pairs
    if p == -5 and h == 1:
        pairs = [(8, -3)] + pairs
    return pairs


def way_up(d, h):
    if d == 8:
        return -3 if h == 0 else 3
    return PARENT[d] - d


PEERS = (
    [(dx, dy, 0, 0) for dx, dy in XY]
    + [(0, 0, d, 0) for d in (5, -5, 3, -3, 2, -2, 1, -1)]
    + [(0, 0, d, 1) for d in FIRST]
    + [(0, 0, 0, 1)]
)
N_SEMS = 160


def kernel(
    feat, weight, cot, blocks, counts, tiles, act_out, fg_out, wg_out,
    tile_v, dense, gath, blk_v, inv_v, inv_s, w_all, cot_v, cot_h, leaf_s, leaf_r, part, first_s, first_r,
    sib_s, sib_r, agg, act_s, act_r, slope_s, slope_p, slope_t, spread_t, back_s, back_r, wgp, wg_s, wg_r, wg_t, wc_s,
    wc_r, wz, wt, load_sem, inv_sem, send_sem, recv_sem,
):
    i = lax.axis_index("row")
    z = lax.axis_index("col")
    c = lax.axis_index("dep")
    x, y = lax.rem(i, NX), lax.div(i, NX)

    def row_at(dx, dy):
        return lax.rem(y + (dy + NY), NY) * NX + lax.rem(x + (dx + NX), NX)

    def z_at(d):
        return lax.rem(z + (d + NZ), NZ)

    def device(dx, dy, dz, dc):
        return (row_at(dx, dy), z_at(dz), 1 - c if dc else c)

    def block(at, size=B):
        return pl.ds(pl.multiple_of(at * size, size), size)

    def piece(at, h):
        return pl.ds(pl.multiple_of(at * B + h * HB, HB), HB)

    counter = [0]
    sent = []

    def slots(n):
        counter[0] += n
        return counter[0] - n

    def remote(src, dst, where, send_k, recv_k):
        return pltpu.make_async_remote_copy(
            src_ref=src, dst_ref=dst, send_sem=send_sem.at[send_k], recv_sem=recv_sem.at[recv_k],
            device_id=where, device_id_type=MESH,
        )

    def send(src, dst, where):
        k = slots(1)
        copy = remote(src, dst, where, k, k)
        copy.start()
        sent.append(copy)
        return copy

    def send_to_core(src, dst, z_to, q, k):
        copy = remote(src, dst, (i, z_to, jnp.int32(q)), k + q, k + c)
        copy.start()
        sent.append(copy)

    def expect(dst, k):
        return remote(dst, dst, (i, z, 1 - c), k, k)

    loads = []

    def load(src, dst):
        copy = pltpu.make_async_copy(src, dst, load_sem.at[len(loads)])
        copy.start()
        loads.append(copy)
        return copy

    own = block(i)
    got_blocks = load(blocks.at[0, 0], blk_v)
    got_feat = load(feat.at[:, block(c)], gath.at[own])
    own_w = load(weight, w_all.at[c])
    own_cot = load(cot, cot_v)
    got_tiles = [load(tiles.at[0, 0, pl.ds(q * 32, 32)], tile_v.at[pl.ds(q * 32, 32)]) for q in range(4)]
    barrier = pltpu.get_barrier_semaphore()
    for peer in PEERS:
        pl.semaphore_signal(barrier, inc=1, device_id=device(*peer), device_id_type=MESH)

    got_blocks.wait()
    flat = blk_v[0:1, :] * BPP + blk_v[1:2, :]
    lane = lax.broadcasted_iota(jnp.int32, (1, B), 1)
    flat = jnp.where(lane < jnp.broadcast_to(counts[...], (1, B)), flat, -1)
    flat = jnp.broadcast_to(flat, (B, B)).T
    slot = lax.broadcasted_iota(jnp.int32, (B, B), 0) - B
    place = lax.broadcasted_iota(jnp.int32, (B, B), 1)
    inv_v[...] = jnp.zeros_like(inv_v)
    for h in range(2):
        hit = jnp.where(flat == place + h * B, slot, 0)
        inv_v[h : h + 1, :] = jnp.clip(jnp.sum(hit, axis=0, keepdims=True) + B, 0, B)
    inv_copy = pltpu.make_async_copy(inv_v, inv_s, inv_sem)
    inv_copy.start()
    tile_v[B] = jnp.zeros((B, B), BF16)
    got_feat.wait()
    own_w.wait()
    own_cot.wait()
    cot_h[c] = cot_v[block(c, HB), :]

    pl.semaphore_wait(barrier, len(PEERS))

    gathered = [send(gath.at[own], gath.at[own], device(dx, dy, 0, 0)) for dx, dy in XY]
    got_w = send(w_all.at[c], w_all.at[c], device(0, 0, 0, 1))
    got_cot = send(cot_v.at[block(1 - c, HB)], cot_h.at[c], device(0, 0, 0, 1))

    inv_copy.wait()
    for copy in got_tiles:
        copy.wait()

    @pl.loop(0, BPP)
    def _(r):
        rows = block(r)
        for col in range(BPP):
            at = r * BPP + col
            dense[rows, col * B : (col + 1) * B] = tile_v[inv_s[lax.div(at, B), lax.rem(at, B)]]

    for copy in gathered:
        copy.wait_recv()

    def chunk(d):
        return jnp.dot(dense[block(z_at(-d)), :], gath[...], preferred_element_type=F32)

    halves_of = [pl.ds(h * HB, HB) for h in range(2)]
    leaf_copy = {}

    def send_leaf(d, h):
        k = LEAVES.index(d)
        leaf_copy[d, h] = send(
            leaf_s.at[k, halves_of[h]], leaf_r.at[k, halves_of[h]], device(0, 0, way_up(d, h), 0)
        )

    for k, d in enumerate(LEAVES):
        leaf_s[k] = chunk(d).astype(BF16)
        for h in range(2):
            send_leaf(d, h)
    for k, p in enumerate(FIRST):
        value = chunk(p)
        if p in INNER:
            part[k] = value
        else:
            first_s[k] = value.astype(BF16)
    part[len(FIRST)] = chunk(0)
    first_k = {p: slots(2) for p in FIRST}

    def send_first(p, h):
        k = FIRST.index(p)
        if p in INNER:
            total = part[k, halves_of[h], :]
            for d, _ in children(p, h):
                leaf_copy[d, h].wait_recv()
                total = total + leaf_r[LEAVES.index(d), halves_of[h], :].astype(F32)
            first_s[k, halves_of[h], :] = total.astype(BF16)
        send_to_core(first_s.at[k, halves_of[h]], first_r.at[k, c], z_at(-p), h, first_k[p])

    sib_s[...] = part[len(FIRST), block(1 - c, HB), :].astype(BF16)
    sib_copy = send(sib_s, sib_r, device(0, 0, 0, 1))
    agg[c] = part[len(FIRST), block(c, HB), :]
    for h in range(2):
        for p in (1, -1) + INNER:
            send_first(p, h)
    sib_copy.wait_recv()
    agg[1 - c] = sib_r[...].astype(F32)
    got_w.wait_recv()
    got_cot.wait_recv()
    for p in (1, -1, 2, -2, 5, -5):
        for q in range(2):
            expect(first_r.at[FIRST.index(p), q], first_k[p] + q).wait_recv()
    halves = []
    for h in range(2):
        total = agg[h]
        for k in range(len(FIRST)):
            total = total + first_r[k, h].astype(F32)
        halves.append(total.astype(BF16))

    slopes = []
    for u in range(2):
        pre = sum(
            jnp.dot(halves[h], w_all[u, h * B : (h + 1) * B, :], preferred_element_type=F32) for h in range(2)
        )
        squash = jnp.tanh(pre)
        act_s[u] = squash.astype(BF16)
        slopes.append((cot_h[u].astype(F32) * (1.0 - squash * squash)).astype(BF16))
    for h in range(2):
        back = sum(
            lax.dot_general(
                slopes[u], w_all[u, h * B : (h + 1) * B, :], (((1,), (1,)), ((), ())), preferred_element_type=F32
            )
            for u in range(2)
        )
        slope_s[h] = back.astype(BF16)

    here = piece(z, c)
    out_k = {p: slots(2) for p in FIRST}
    for p in FIRST:
        for q in range(2):
            send_to_core(slope_s.at[q], slope_p.at[here], z_at(p), q, out_k[p])
    near = send(slope_s.at[1 - c], slope_p.at[here], device(0, 0, 0, 1))
    slope_p[here, :] = slope_s[c]

    for u in range(2):
        for h in range(2):
            wgp[u, h * B : (h + 1) * B, :] = lax.dot_general(
                halves[h], slopes[u], (((0,), (0,)), ((), ())), preferred_element_type=F32
            )
    wg_s[...] = wgp[1 - c].astype(BF16)
    wg_copy = send(wg_s, wg_r, device(0, 0, 0, 1))
    act_copy = send(act_s.at[1 - c], act_r, device(0, 0, 0, 1))
    act_out[block(c, HB), :] = act_s[c]

    leaf_out = {}

    def forward(p, h):
        rows = piece(z_at(-p), h)
        expect(slope_p.at[rows], out_k[p] + h).wait_recv()
        for d, way in children(p, h):
            leaf_out[d, h] = send(slope_p.at[rows], slope_p.at[rows], device(0, 0, way, 0))

    wg_copy.wait_recv()
    wg_t[...] = wgp[c] + wg_r[...].astype(F32)
    wc_s[...] = wg_t[...].astype(BF16)
    wc_copy = [
        send(wc_s.at[block(row_at(dx, dy), 16)], wc_r.at[k], device(dx, dy, 0, 0))
        for k, (dx, dy) in enumerate(XY)
    ]
    for p in (2, -2, 5, -5):
        forward(p, 0)
    for copy in wc_copy:
        copy.wait_recv()
    total = wg_t[block(i, 16), :]
    for k in range(len(XY)):
        total = total + wc_r[k].astype(F32)
    wz[z] = total.astype(BF16)
    wz_first = {p: send(wz.at[z], wz.at[z], device(0, 0, p, 0)) for p in FIRST}

    for p in (2, -2, 5, -5):
        forward(p, 1)

    act_copy.wait_recv()
    act_out[block(1 - c, HB), :] = act_r[...]

    def turn(d):
        slope_t[:, block(z_at(-d))] = slope_p[block(z_at(-d)), :].T

    near.wait_recv()
    turn(0)
    for p in (1, -1):
        for q in range(2):
            expect(slope_p.at[piece(z_at(-p), q)], out_k[p] + q).wait_recv()
        turn(p)
    for p in INNER:
        turn(p)
    wz_leaf = {}
    for p in FIRST:
        wz_first[p].wait_recv()
        at = z_at(-p)
        for d, way in children(p, 0):
            wz_leaf[d] = send(wz.at[at], wz.at[at], device(0, 0, way, 0))
    for d in LEAVES[::-1]:
        for h in range(2):
            leaf_out[d, h].wait_recv()
        turn(d)

    back_copy = []
    for dy in (2, 1, -1, 0):
        group = lax.rem(y + (dy + NY), NY)
        value = jnp.dot(slope_t[...], dense[:, block(group, NX * B)], preferred_element_type=F32)
        for k in range(NX):
            back_s[group * NX + k] = value[:, k * B : (k + 1) * B].astype(BF16)
            if dy == 0:
                spread_t[k] = value[:, k * B : (k + 1) * B]
        for dx in (2, 1, -1, 0):
            if (dx, dy) != (0, 0):
                k = XY.index((dx, dy))
                back_copy.append(send(back_s.at[row_at(dx, dy)], back_r.at[k], device(dx, dy, 0, 0)))

    for d in LEAVES:
        wz_leaf[d].wait_recv()
    total = wz[0].astype(F32)
    for k in range(1, NZ):
        total = total + wz[k].astype(F32)
    wt[block(i, 16), :] = total
    wt_copy = [
        send(wt.at[block(i, 16)], wt.at[block(i, 16)], device(dx, dy, 0, 0)) for dx, dy in XY
    ]

    for copy in back_copy:
        copy.wait_recv()
    total = spread_t[x]
    for k in range(len(XY)):
        total = total + back_r[k].astype(F32)
    fg_out[...] = total.T.astype(BF16)

    for copy in wt_copy:
        copy.wait_recv()
    wg_out[...] = wt[...]
    for copy in sent:
        copy.wait_send()


def hand_on(*refs):
    n = len(refs) // 2
    for k in range(n):
        refs[n + k][...] = refs[k][...]


def per_device(features, weight, tiles, tile_blocks, tile_counts, cotangent):
    vmem = pl.BlockSpec(memory_space=pltpu.VMEM)
    hbm = pl.BlockSpec(memory_space=pl.ANY)
    n_xy = len(XY)
    scratch = [
        pltpu.VMEM((B + 1, B, B), BF16),
        pltpu.VMEM((NODES, NODES), BF16),
        pltpu.VMEM((NODES, B), BF16),
        pltpu.VMEM((2, B), jnp.int32),
        pltpu.VMEM((8, B), jnp.int32),
        pltpu.SMEM((8, B), jnp.int32),
        pltpu.VMEM((2, 2 * B, B), BF16),
        pltpu.VMEM((B, B), BF16),
        pltpu.VMEM((2, HB, B), BF16),
        pltpu.VMEM((9, B, B), BF16),
        pltpu.VMEM((9, B, B), BF16),
        pltpu.VMEM((7, B, B), F32),
        pltpu.VMEM((6, B, B), BF16),
        pltpu.VMEM((6, 2, HB, B), BF16),
        pltpu.VMEM((HB, B), BF16),
        pltpu.VMEM((HB, B), BF16),
        pltpu.VMEM((2, HB, B), F32),
        pltpu.VMEM((2, HB, B), BF16),
        pltpu.VMEM((HB, B), BF16),
        pltpu.VMEM((2, HB, B), BF16),
        pltpu.VMEM((NODES, B), BF16),
        pltpu.VMEM((B, NODES), BF16),
        pltpu.VMEM((NX, B, B), F32),
        pltpu.VMEM((BPP, B, B), BF16),
        pltpu.VMEM((n_xy, B, B), BF16),
        pltpu.VMEM((2, 2 * B, B), F32),
        pltpu.VMEM((2 * B, B), BF16),
        pltpu.VMEM((2 * B, B), BF16),
        pltpu.VMEM((2 * B, B), F32),
        pltpu.VMEM((2 * B, B), BF16),
        pltpu.VMEM((n_xy, 16, B), BF16),
        pltpu.VMEM((NZ, 16, B), BF16),
        pltpu.VMEM((2 * B, B), F32),
        pltpu.SemaphoreType.DMA((8,)),
        pltpu.SemaphoreType.DMA,
        pltpu.SemaphoreType.DMA((N_SEMS,)),
        pltpu.SemaphoreType.DMA((N_SEMS,)),
    ]
    out_shape = (
        jax.ShapeDtypeStruct((B, B), BF16),
        jax.ShapeDtypeStruct((B, B), BF16),
        jax.ShapeDtypeStruct((2 * B, B), F32),
    )
    results = pl.pallas_call(
        kernel,
        out_shape=out_shape,
        in_specs=[hbm, hbm, hbm, hbm, vmem, hbm],
        out_specs=(vmem, vmem, vmem),
        scratch_shapes=scratch,
        compiler_params=pltpu.CompilerParams(collective_id=0, has_side_effects=True, vmem_limit_bytes=56 * 2**20),
        cost_estimate=pl.CostEstimate(flops=4 * NODES * NODES * B, bytes_accessed=2**23, transcendentals=B * B),
        name="gcn",
    )(features, weight, cotangent, tile_blocks, tile_counts, tiles)
    results = pl.pallas_call(
        hand_on,
        out_shape=out_shape,
        in_specs=[vmem] * 3,
        out_specs=(vmem, vmem, vmem),
        cost_estimate=pl.CostEstimate(flops=0, bytes_accessed=2**19, transcendentals=0),
        name="hand_on",
    )(*results)
    return tuple(results)


def solution(mesh):
    return jax.shard_map(
        per_device,
        mesh=mesh,
        in_specs=(
            P(("col", "row"), None),
            P(None, "dep"),
            P("row", "col", None, None, None),
            P("row", "col", None, None),
            P("row", "col"),
            P(("row", "col"), "dep"),
        ),
        out_specs=(P(("row", "col"), "dep"), P(("col", "row"), "dep"), P(None, "dep")),
        check_vma=False,
    )
```

```python
import functools

import jax
import jax.numpy as jnp
from jax import lax
from jax.experimental import pallas as pl
from jax.experimental.pallas import tpu as pltpu
from jax.sharding import PartitionSpec as P

MESH = pl.DeviceIdType.MESH
F32, BF16 = jnp.float32, jnp.bfloat16
B = 128
BPP = 16
NODES = BPP * B
HB = B // 2
NX, NY, NZ = 4, 4, 16
XY = sorted(
    [(dx, dy) for dx in (0, 1, -1, 2) for dy in (0, 1, -1, 2) if (dx, dy) != (0, 0)],
    key=lambda o: -(abs(o[0]) + abs(o[1])),
)
FIRST = (5, -5, 2, -2, 1, -1)
INNER = (5, -5, 2, -2)
LEAVES = (8, 7, -7, 6, -6, 4, -4, 3, -3)
CHILDREN = {5: (7, 6, 4), -5: (-7, -6, -4), 2: (3,), -2: (-3,), 1: (), -1: ()}
PARENT = {d: p for p, ds in CHILDREN.items() for d in ds}


def children(p, h):
    pairs = [(d, d - p) for d in CHILDREN[p]]
    if p == 5 and h == 0:
        pairs = [(8, 3)] + pairs
    if p == -5 and h == 1:
        pairs = [(8, -3)] + pairs
    return pairs


def way_up(d, h):
    if d == 8:
        return -3 if h == 0 else 3
    return PARENT[d] - d


PEERS = (
    [(dx, dy, 0, 0) for dx, dy in XY]
    + [(0, 0, d, 0) for d in (5, -5, 3, -3, 2, -2, 1, -1)]
    + [(0, 0, d, 1) for d in FIRST]
    + [(0, 0, 0, 1)]
)
N_SEMS = 160


def kernel(
    feat, weight, cot, blocks, counts, tiles, act_out, fg_out, wg_out,
    tile_v, dense, gath, blk_v, inv_v, inv_s, w_all, cot_v, cot_h, leaf_s, leaf_r, part, first_s, first_r,
    sib_s, sib_r, agg, act_s, act_r, slope_s, slope_p, slope_t, spread_t, back_s, back_r, wgp, wg_s, wg_r, wg_t, wc_s,
    wc_r, wz, wt, load_sem, inv_sem, send_sem, recv_sem,
):
    i = lax.axis_index("row")
    z = lax.axis_index("col")
    c = lax.axis_index("dep")
    x, y = lax.rem(i, NX), lax.div(i, NX)

    def row_at(dx, dy):
        return lax.rem(y + (dy + NY), NY) * NX + lax.rem(x + (dx + NX), NX)

    def z_at(d):
        return lax.rem(z + (d + NZ), NZ)

    def device(dx, dy, dz, dc):
        return (row_at(dx, dy), z_at(dz), 1 - c if dc else c)

    def block(at, size=B):
        return pl.ds(pl.multiple_of(at * size, size), size)

    def piece(at, h):
        return pl.ds(pl.multiple_of(at * B + h * HB, HB), HB)

    counter = [0]
    sent = []

    def slots(n):
        counter[0] += n
        return counter[0] - n

    def remote(src, dst, where, send_k, recv_k):
        return pltpu.make_async_remote_copy(
            src_ref=src, dst_ref=dst, send_sem=send_sem.at[send_k], recv_sem=recv_sem.at[recv_k],
            device_id=where, device_id_type=MESH,
        )

    def send(src, dst, where):
        k = slots(1)
        copy = remote(src, dst, where, k, k)
        copy.start()
        sent.append(copy)
        return copy

    def settle():
        for copy in sent:
            copy.wait_send()
        sent.clear()

    def send_to_core(src, dst, z_to, q, k):
        copy = remote(src, dst, (i, z_to, jnp.int32(q)), k + q, k + c)
        copy.start()
        sent.append(copy)

    def expect(dst, k):
        return remote(dst, dst, (i, z, 1 - c), k, k)

    loads = []

    def load(src, dst):
        copy = pltpu.make_async_copy(src, dst, load_sem.at[len(loads)])
        copy.start()
        loads.append(copy)
        return copy

    own = block(i)
    got_blocks = load(blocks.at[0, 0], blk_v)
    got_feat = load(feat.at[:, block(c)], gath.at[own])
    own_w = load(weight, w_all.at[c])
    own_cot = load(cot, cot_v)
    got_tiles = [load(tiles.at[0, 0, pl.ds(q * 32, 32)], tile_v.at[pl.ds(q * 32, 32)]) for q in range(4)]
    barrier = pltpu.get_barrier_semaphore()
    for peer in PEERS:
        pl.semaphore_signal(barrier, inc=1, device_id=device(*peer), device_id_type=MESH)

    got_blocks.wait()
    flat = blk_v[0:1, :] * BPP + blk_v[1:2, :]
    lane = lax.broadcasted_iota(jnp.int32, (1, B), 1)
    flat = jnp.where(lane < jnp.broadcast_to(counts[...], (1, B)), flat, -1)
    flat = jnp.broadcast_to(flat, (B, B)).T
    slot = lax.broadcasted_iota(jnp.int32, (B, B), 0) - B
    place = lax.broadcasted_iota(jnp.int32, (B, B), 1)
    inv_v[...] = jnp.zeros_like(inv_v)
    for h in range(2):
        hit = jnp.where(flat == place + h * B, slot, 0)
        inv_v[h : h + 1, :] = jnp.clip(jnp.sum(hit, axis=0, keepdims=True) + B, 0, B)
    inv_copy = pltpu.make_async_copy(inv_v, inv_s, inv_sem)
    inv_copy.start()
    tile_v[B] = jnp.zeros((B, B), BF16)
    got_feat.wait()
    own_w.wait()
    own_cot.wait()
    cot_h[c] = cot_v[block(c, HB), :]

    pl.semaphore_wait(barrier, len(PEERS))

    gathered = [send(gath.at[own], gath.at[own], device(dx, dy, 0, 0)) for dx, dy in XY]
    got_w = send(w_all.at[c], w_all.at[c], device(0, 0, 0, 1))
    got_cot = send(cot_v.at[block(1 - c, HB)], cot_h.at[c], device(0, 0, 0, 1))

    inv_copy.wait()
    for copy in got_tiles:
        copy.wait()

    @pl.loop(0, BPP)
    def _(r):
        rows = block(r)
        for col in range(BPP):
            at = r * BPP + col
            dense[rows, col * B : (col + 1) * B] = tile_v[inv_s[lax.div(at, B), lax.rem(at, B)]]

    for copy in gathered:
        copy.wait_recv()

    def chunk(d):
        return jnp.dot(dense[block(z_at(-d)), :], gath[...], preferred_element_type=F32)

    halves_of = [pl.ds(h * HB, HB) for h in range(2)]
    leaf_copy = {}

    def send_leaf(d, h):
        k = LEAVES.index(d)
        leaf_copy[d, h] = send(
            leaf_s.at[k, halves_of[h]], leaf_r.at[k, halves_of[h]], device(0, 0, way_up(d, h), 0)
        )

    for k, d in enumerate(LEAVES):
        leaf_s[k] = chunk(d).astype(BF16)
        for h in range(2):
            send_leaf(d, h)
    for k, p in enumerate(FIRST):
        value = chunk(p)
        if p in INNER:
            part[k] = value
        else:
            first_s[k] = value.astype(BF16)
    part[len(FIRST)] = chunk(0)
    first_k = {p: slots(2) for p in FIRST}

    def send_first(p, h):
        k = FIRST.index(p)
        if p in INNER:
            total = part[k, halves_of[h], :]
            for d, _ in children(p, h):
                leaf_copy[d, h].wait_recv()
                total = total + leaf_r[LEAVES.index(d), halves_of[h], :].astype(F32)
            first_s[k, halves_of[h], :] = total.astype(BF16)
        send_to_core(first_s.at[k, halves_of[h]], first_r.at[k, c], z_at(-p), h, first_k[p])

    sib_s[...] = part[len(FIRST), block(1 - c, HB), :].astype(BF16)
    sib_copy = send(sib_s, sib_r, device(0, 0, 0, 1))
    agg[c] = part[len(FIRST), block(c, HB), :]
    for h in range(2):
        for p in (1, -1) + INNER:
            send_first(p, h)
    early = sent[:-12]
    for copy in early:
        copy.wait_send()
    del sent[:-12]
    sib_copy.wait_recv()
    agg[1 - c] = sib_r[...].astype(F32)
    got_w.wait_recv()
    got_cot.wait_recv()
    for p in (1, -1, 2, -2, 5, -5):
        for q in range(2):
            expect(first_r.at[FIRST.index(p), q], first_k[p] + q).wait_recv()
    halves = []
    for h in range(2):
        total = agg[h]
        for k in range(len(FIRST)):
            total = total + first_r[k, h].astype(F32)
        halves.append(total.astype(BF16))

    slopes = []
    for u in range(2):
        pre = sum(
            jnp.dot(halves[h], w_all[u, h * B : (h + 1) * B, :], preferred_element_type=F32) for h in range(2)
        )
        squash = jnp.tanh(pre)
        act_s[u] = squash.astype(BF16)
        slopes.append((cot_h[u].astype(F32) * (1.0 - squash * squash)).astype(BF16))
    for h in range(2):
        back = sum(
            lax.dot_general(
                slopes[u], w_all[u, h * B : (h + 1) * B, :], (((1,), (1,)), ((), ())), preferred_element_type=F32
            )
            for u in range(2)
        )
        slope_s[h] = back.astype(BF16)

    here = piece(z, c)
    out_k = {p: slots(2) for p in FIRST}
    for p in FIRST:
        for q in range(2):
            send_to_core(slope_s.at[q], slope_p.at[here], z_at(p), q, out_k[p])
    near = send(slope_s.at[1 - c], slope_p.at[here], device(0, 0, 0, 1))
    slope_p[here, :] = slope_s[c]

    for u in range(2):
        for h in range(2):
            wgp[u, h * B : (h + 1) * B, :] = lax.dot_general(
                halves[h], slopes[u], (((0,), (0,)), ((), ())), preferred_element_type=F32
            )
    wg_s[...] = wgp[1 - c].astype(BF16)
    wg_copy = send(wg_s, wg_r, device(0, 0, 0, 1))
    act_copy = send(act_s.at[1 - c], act_r, device(0, 0, 0, 1))
    act_out[block(c, HB), :] = act_s[c]

    leaf_out = {}

    def forward(p, h):
        rows = piece(z_at(-p), h)
        expect(slope_p.at[rows], out_k[p] + h).wait_recv()
        for d, way in children(p, h):
            leaf_out[d, h] = send(slope_p.at[rows], slope_p.at[rows], device(0, 0, way, 0))

    wg_copy.wait_recv()
    wg_t[...] = wgp[c] + wg_r[...].astype(F32)
    wc_s[...] = wg_t[...].astype(BF16)
    wc_copy = [
        send(wc_s.at[block(row_at(dx, dy), 16)], wc_r.at[k], device(dx, dy, 0, 0))
        for k, (dx, dy) in enumerate(XY)
    ]
    early = sent[:-15]
    for copy in early:
        copy.wait_send()
    del sent[:-15]
    for p in (2, -2, 5, -5):
        forward(p, 0)
    for copy in wc_copy:
        copy.wait_recv()
    total = wg_t[block(i, 16), :]
    for k in range(len(XY)):
        total = total + wc_r[k].astype(F32)
    wz[z] = total.astype(BF16)
    wz_first = {p: send(wz.at[z], wz.at[z], device(0, 0, p, 0)) for p in FIRST}

    for p in (2, -2, 5, -5):
        forward(p, 1)

    act_copy.wait_recv()
    act_out[block(1 - c, HB), :] = act_r[...]

    def turn(d):
        slope_t[:, block(z_at(-d))] = slope_p[block(z_at(-d)), :].T

    near.wait_recv()
    turn(0)
    for p in (1, -1):
        for q in range(2):
            expect(slope_p.at[piece(z_at(-p), q)], out_k[p] + q).wait_recv()
        turn(p)
    for p in INNER:
        turn(p)
    wz_leaf = {}
    for p in FIRST:
        wz_first[p].wait_recv()
        at = z_at(-p)
        for d, way in children(p, 0):
            wz_leaf[d] = send(wz.at[at], wz.at[at], device(0, 0, way, 0))
    settle()
    for d in LEAVES[::-1]:
        for h in range(2):
            leaf_out[d, h].wait_recv()
        turn(d)

    back_copy = []
    for dy in (2, 1, -1, 0):
        if dy == 0:
            for d in LEAVES:
                wz_leaf[d].wait_recv()
            grad = wz[0].astype(F32)
            for k in range(1, NZ):
                grad = grad + wz[k].astype(F32)
            wt[block(i, 16), :] = grad
            wt_copy = [
                send(wt.at[block(i, 16)], wt.at[block(i, 16)], device(dx, dy, 0, 0)) for dx, dy in XY
            ]
        group = lax.rem(y + (dy + NY), NY)
        value = jnp.dot(slope_t[...], dense[:, block(group, NX * B)], preferred_element_type=F32)
        for k in range(NX):
            back_s[group * NX + k] = value[:, k * B : (k + 1) * B].astype(BF16)
            if dy == 0:
                spread_t[k] = value[:, k * B : (k + 1) * B]
        for dx in (2, 1, -1, 0):
            if (dx, dy) != (0, 0):
                k = XY.index((dx, dy))
                back_copy.append(send(back_s.at[row_at(dx, dy)], back_r.at[k], device(dx, dy, 0, 0)))

    for copy in back_copy:
        copy.wait_recv()
    total = spread_t[x]
    for k in range(len(XY)):
        total = total + back_r[k].astype(F32)
    fg_out[...] = total.T.astype(BF16)

    for copy in wt_copy:
        copy.wait_recv()
    wg_out[...] = wt[...]
    settle()


def hand_on(*refs):
    n = len(refs) // 2
    for k in range(n):
        refs[n + k][...] = refs[k][...]


def per_device(features, weight, tiles, tile_blocks, tile_counts, cotangent):
    vmem = pl.BlockSpec(memory_space=pltpu.VMEM)
    hbm = pl.BlockSpec(memory_space=pl.ANY)
    n_xy = len(XY)
    scratch = [
        pltpu.VMEM((B + 1, B, B), BF16),
        pltpu.VMEM((NODES, NODES), BF16),
        pltpu.VMEM((NODES, B), BF16),
        pltpu.VMEM((2, B), jnp.int32),
        pltpu.VMEM((8, B), jnp.int32),
        pltpu.SMEM((8, B), jnp.int32),
        pltpu.VMEM((2, 2 * B, B), BF16),
        pltpu.VMEM((B, B), BF16),
        pltpu.VMEM((2, HB, B), BF16),
        pltpu.VMEM((9, B, B), BF16),
        pltpu.VMEM((9, B, B), BF16),
        pltpu.VMEM((7, B, B), F32),
        pltpu.VMEM((6, B, B), BF16),
        pltpu.VMEM((6, 2, HB, B), BF16),
        pltpu.VMEM((HB, B), BF16),
        pltpu.VMEM((HB, B), BF16),
        pltpu.VMEM((2, HB, B), F32),
        pltpu.VMEM((2, HB, B), BF16),
        pltpu.VMEM((HB, B), BF16),
        pltpu.VMEM((2, HB, B), BF16),
        pltpu.VMEM((NODES, B), BF16),
        pltpu.VMEM((B, NODES), BF16),
        pltpu.VMEM((NX, B, B), F32),
        pltpu.VMEM((BPP, B, B), BF16),
        pltpu.VMEM((n_xy, B, B), BF16),
        pltpu.VMEM((2, 2 * B, B), F32),
        pltpu.VMEM((2 * B, B), BF16),
        pltpu.VMEM((2 * B, B), BF16),
        pltpu.VMEM((2 * B, B), F32),
        pltpu.VMEM((2 * B, B), BF16),
        pltpu.VMEM((n_xy, 16, B), BF16),
        pltpu.VMEM((NZ, 16, B), BF16),
        pltpu.VMEM((2 * B, B), F32),
        pltpu.SemaphoreType.DMA((8,)),
        pltpu.SemaphoreType.DMA,
        pltpu.SemaphoreType.DMA((N_SEMS,)),
        pltpu.SemaphoreType.DMA((N_SEMS,)),
    ]
    out_shape = (
        jax.ShapeDtypeStruct((B, B), BF16),
        jax.ShapeDtypeStruct((B, B), BF16),
        jax.ShapeDtypeStruct((2 * B, B), F32),
    )
    results = pl.pallas_call(
        kernel,
        out_shape=(pltpu.VMEM((B, B), BF16), pltpu.VMEM((B, B), BF16), pltpu.VMEM((2 * B, B), F32)),
        in_specs=[hbm, hbm, hbm, hbm, vmem, hbm],
        out_specs=(vmem, vmem, vmem),
        scratch_shapes=scratch,
        compiler_params=pltpu.CompilerParams(collective_id=0, has_side_effects=True, vmem_limit_bytes=56 * 2**20),
        cost_estimate=pl.CostEstimate(flops=4 * NODES * NODES * B, bytes_accessed=2**23, transcendentals=B * B),
        name="gcn",
    )(features, weight, cotangent, tile_blocks, tile_counts, tiles)
    results = pl.pallas_call(
        hand_on,
        out_shape=out_shape,
        in_specs=[vmem] * 3,
        out_specs=(vmem, vmem, vmem),
        cost_estimate=pl.CostEstimate(flops=0, bytes_accessed=2**19, transcendentals=0),
        name="hand_on",
    )(*[pltpu.with_memory_space_constraint(r, pltpu.VMEM) for r in results])
    return tuple(results)


def solution(mesh):
    return jax.shard_map(
        per_device,
        mesh=mesh,
        in_specs=(
            P(("col", "row"), None),
            P(None, "dep"),
            P("row", "col", None, None, None),
            P("row", "col", None, None),
            P("row", "col"),
            P(("row", "col"), "dep"),
        ),
        out_specs=(P(("row", "col"), "dep"), P(("col", "row"), "dep"), P(None, "dep")),
        check_vma=False,
    )
```

```python
import functools

import jax
import jax.numpy as jnp
from jax import lax
from jax.experimental import pallas as pl
from jax.experimental.pallas import tpu as pltpu
from jax.sharding import PartitionSpec as P

MESH = pl.DeviceIdType.MESH
F32, BF16 = jnp.float32, jnp.bfloat16
B = 128
BPP = 16
NODES = BPP * B
HB = B // 2
NX, NY, NZ = 4, 4, 16
XY = sorted(
    [(dx, dy) for dx in (0, 1, -1, 2) for dy in (0, 1, -1, 2) if (dx, dy) != (0, 0)],
    key=lambda o: -(abs(o[0]) + abs(o[1])),
)
TREE = {5: (7, 6, 4), 2: (3,), 1: ()}
FAR = max(TREE)
CHILDREN = {s * p: tuple(s * d for d in ds) for p, ds in TREE.items() for s in (1, -1)}
FIRST = tuple(CHILDREN)
INNER = tuple(p for p in FIRST if CHILDREN[p] or abs(p) == FAR)
NEAR = tuple(p for p in FIRST if p not in INNER)
PARENT = {d: p for p, ds in CHILDREN.items() for d in ds}
LEAVES = (8,) + tuple(sorted(PARENT, key=lambda d: (-abs(d), -d)))


def children(p, h):
    pairs = [(d, d - p) for d in CHILDREN[p]]
    if p == FAR and h == 0:
        pairs = [(8, 8 - FAR)] + pairs
    if p == -FAR and h == 1:
        pairs = [(8, FAR - 8)] + pairs
    return pairs


def way_up(d, h):
    if d == 8:
        return FAR - 8 if h == 0 else 8 - FAR
    return PARENT[d] - d


PEERS = sorted(
    [(dx, dy, 0, 0) for dx, dy in XY]
    + [(0, 0, d, 0) for d in sorted({w for p in FIRST for h in range(2) for _, w in children(p, h)} | set(FIRST))]
    + [(0, 0, d, 1) for d in FIRST]
    + [(0, 0, 0, 1)],
    key=lambda o: -sum(map(abs, o)),
)
N_SEMS = 160


def kernel(
    feat, weight, cot, blocks, counts, tiles, act_out, fg_out, wg_out,
    tile_v, dense, gath, blk_v, inv_v, inv_s, w_all, cot_v, cot_h, leaf_s, leaf_r, part, first_s, first_r,
    sib_s, sib_r, agg, act_s, act_r, slope_s, slope_p, slope_t, spread_t, back_s, back_r, wgp, wg_s, wg_r, wg_t, wc_s,
    wc_r, wz, wt, load_sem, inv_sem, send_sem, recv_sem,
):
    i = lax.axis_index("row")
    z = lax.axis_index("col")
    c = lax.axis_index("dep")
    x, y = lax.rem(i, NX), lax.div(i, NX)

    def row_at(dx, dy):
        return lax.rem(y + (dy + NY), NY) * NX + lax.rem(x + (dx + NX), NX)

    def z_at(d):
        return lax.rem(z + (d + NZ), NZ)

    def device(dx, dy, dz, dc):
        return (row_at(dx, dy), z_at(dz), 1 - c if dc else c)

    def block(at, size=B):
        return pl.ds(pl.multiple_of(at * size, size), size)

    def piece(at, h):
        return pl.ds(pl.multiple_of(at * B + h * HB, HB), HB)

    counter = [0]
    sent = []

    def slots(n):
        counter[0] += n
        return counter[0] - n

    def remote(src, dst, where, send_k, recv_k):
        return pltpu.make_async_remote_copy(
            src_ref=src, dst_ref=dst, send_sem=send_sem.at[send_k], recv_sem=recv_sem.at[recv_k],
            device_id=where, device_id_type=MESH,
        )

    def send(src, dst, where):
        k = slots(1)
        copy = remote(src, dst, where, k, k)
        copy.start()
        sent.append(copy)
        return copy

    def settle():
        for copy in sent:
            copy.wait_send()
        sent.clear()

    def send_to_core(src, dst, z_to, q, k):
        copy = remote(src, dst, (i, z_to, jnp.int32(q)), k + q, k + c)
        copy.start()
        sent.append(copy)

    def expect(dst, k):
        return remote(dst, dst, (i, z, 1 - c), k, k)

    barrier = pltpu.get_barrier_semaphore()
    for peer in PEERS:
        pl.semaphore_signal(barrier, inc=1, device_id=device(*peer), device_id_type=MESH)
    loads = []

    def load(src, dst):
        copy = pltpu.make_async_copy(src, dst, load_sem.at[len(loads)])
        copy.start()
        loads.append(copy)
        return copy

    own = block(i)
    got_blocks = load(blocks.at[0, 0], blk_v)
    got_feat = load(feat.at[:, block(c)], gath.at[own])
    own_w = load(weight, w_all.at[c])
    own_cot = load(cot, cot_v)
    got_tiles = [load(tiles.at[0, 0, pl.ds(q * 32, 32)], tile_v.at[pl.ds(q * 32, 32)]) for q in range(4)]

    got_blocks.wait()
    flat = blk_v[0:1, :] * BPP + blk_v[1:2, :]
    lane = lax.broadcasted_iota(jnp.int32, (1, B), 1)
    flat = jnp.where(lane < jnp.broadcast_to(counts[...], (1, B)), flat, -1)
    flat = jnp.broadcast_to(flat, (B, B)).T
    slot = lax.broadcasted_iota(jnp.int32, (B, B), 0) - B
    place = lax.broadcasted_iota(jnp.int32, (B, B), 1)
    inv_v[...] = jnp.zeros_like(inv_v)
    for h in range(2):
        hit = jnp.where(flat == place + h * B, slot, 0)
        inv_v[h : h + 1, :] = jnp.clip(jnp.sum(hit, axis=0, keepdims=True) + B, 0, B)
    inv_copy = pltpu.make_async_copy(inv_v, inv_s, inv_sem)
    inv_copy.start()
    tile_v[B] = jnp.zeros((B, B), BF16)
    got_feat.wait()
    own_w.wait()
    own_cot.wait()
    cot_h[c] = cot_v[block(c, HB), :]

    pl.semaphore_wait(barrier, len(PEERS))

    gathered = [send(gath.at[own], gath.at[own], device(dx, dy, 0, 0)) for dx, dy in XY]
    got_w = send(w_all.at[c], w_all.at[c], device(0, 0, 0, 1))
    got_cot = send(cot_v.at[block(1 - c, HB)], cot_h.at[c], device(0, 0, 0, 1))

    inv_copy.wait()
    for copy in got_tiles:
        copy.wait()

    @pl.loop(0, BPP)
    def _(r):
        rows = block(r)
        for col in range(BPP):
            at = r * BPP + col
            dense[rows, col * B : (col + 1) * B] = tile_v[inv_s[lax.div(at, B), lax.rem(at, B)]]

    for copy in gathered:
        copy.wait_recv()

    def chunk(d):
        return jnp.dot(dense[block(z_at(-d)), :], gath[...], preferred_element_type=F32)

    halves_of = [pl.ds(h * HB, HB) for h in range(2)]
    leaf_copy = {}

    def send_leaf(d, h):
        k = LEAVES.index(d)
        leaf_copy[d, h] = send(
            leaf_s.at[k, halves_of[h]], leaf_r.at[k, halves_of[h]], device(0, 0, way_up(d, h), 0)
        )

    for k, d in enumerate(LEAVES):
        leaf_s[k] = chunk(d).astype(BF16)
        for h in range(2):
            send_leaf(d, h)
    for k, p in enumerate(FIRST):
        value = chunk(p)
        if p in INNER:
            part[k] = value
        else:
            first_s[k] = value.astype(BF16)
    part[len(FIRST)] = chunk(0)
    first_k = {p: slots(2) for p in FIRST}

    def send_first(p, h):
        k = FIRST.index(p)
        if p in INNER:
            total = part[k, halves_of[h], :]
            for d, _ in children(p, h):
                leaf_copy[d, h].wait_recv()
                total = total + leaf_r[LEAVES.index(d), halves_of[h], :].astype(F32)
            first_s[k, halves_of[h], :] = total.astype(BF16)
        send_to_core(first_s.at[k, halves_of[h]], first_r.at[k, c], z_at(-p), h, first_k[p])

    sib_s[...] = part[len(FIRST), block(1 - c, HB), :].astype(BF16)
    sib_copy = send(sib_s, sib_r, device(0, 0, 0, 1))
    agg[c] = part[len(FIRST), block(c, HB), :]
    for h in range(2):
        for p in NEAR + INNER:
            send_first(p, h)
    early = sent[:-12]
    for copy in early:
        copy.wait_send()
    del sent[:-12]
    sib_copy.wait_recv()
    agg[1 - c] = sib_r[...].astype(F32)
    got_w.wait_recv()
    got_cot.wait_recv()
    for p in FIRST:
        for q in range(2):
            expect(first_r.at[FIRST.index(p), q], first_k[p] + q).wait_recv()
    halves = []
    for h in range(2):
        total = agg[h]
        for k in range(len(FIRST)):
            total = total + first_r[k, h].astype(F32)
        halves.append(total.astype(BF16))

    slopes = []
    for u in range(2):
        pre = sum(
            jnp.dot(halves[h], w_all[u, h * B : (h + 1) * B, :], preferred_element_type=F32) for h in range(2)
        )
        squash = jnp.tanh(pre)
        act_s[u] = squash.astype(BF16)
        slopes.append((cot_h[u].astype(F32) * (1.0 - squash * squash)).astype(BF16))
    for h in range(2):
        back = sum(
            lax.dot_general(
                slopes[u], w_all[u, h * B : (h + 1) * B, :], (((1,), (1,)), ((), ())), preferred_element_type=F32
            )
            for u in range(2)
        )
        slope_s[h] = back.astype(BF16)

    here = piece(z, c)
    out_k = {p: slots(2) for p in FIRST}
    for p in FIRST:
        for q in range(2):
            send_to_core(slope_s.at[q], slope_p.at[here], z_at(p), q, out_k[p])
    near = send(slope_s.at[1 - c], slope_p.at[here], device(0, 0, 0, 1))
    slope_p[here, :] = slope_s[c]

    for u in range(2):
        for h in range(2):
            wgp[u, h * B : (h + 1) * B, :] = lax.dot_general(
                halves[h], slopes[u], (((0,), (0,)), ((), ())), preferred_element_type=F32
            )
    wg_s[...] = wgp[1 - c].astype(BF16)
    wg_copy = send(wg_s, wg_r, device(0, 0, 0, 1))
    act_copy = send(act_s.at[1 - c], act_r, device(0, 0, 0, 1))
    act_out[block(c, HB), :] = act_s[c]

    leaf_out = {}

    def forward(p, h):
        rows = piece(z_at(-p), h)
        expect(slope_p.at[rows], out_k[p] + h).wait_recv()
        for d, way in children(p, h):
            leaf_out[d, h] = send(slope_p.at[rows], slope_p.at[rows], device(0, 0, way, 0))

    wg_copy.wait_recv()
    wg_t[...] = wgp[c] + wg_r[...].astype(F32)
    wc_s[...] = wg_t[...].astype(BF16)
    wc_copy = [
        send(wc_s.at[block(row_at(dx, dy), 16)], wc_r.at[k], device(dx, dy, 0, 0))
        for k, (dx, dy) in enumerate(XY)
    ]
    early = sent[:-15]
    for copy in early:
        copy.wait_send()
    del sent[:-15]
    for p in INNER:
        forward(p, 0)
    for copy in wc_copy:
        copy.wait_recv()
    total = wg_t[block(i, 16), :]
    for k in range(len(XY)):
        total = total + wc_r[k].astype(F32)
    wz[z] = total.astype(BF16)
    wz_first = {p: send(wz.at[z], wz.at[z], device(0, 0, p, 0)) for p in FIRST}

    for p in INNER:
        forward(p, 1)

    act_copy.wait_recv()
    act_out[block(1 - c, HB), :] = act_r[...]

    def turn(d):
        slope_t[:, block(z_at(-d))] = slope_p[block(z_at(-d)), :].T

    near.wait_recv()
    turn(0)
    for p in NEAR:
        for q in range(2):
            expect(slope_p.at[piece(z_at(-p), q)], out_k[p] + q).wait_recv()
        turn(p)
    for p in INNER:
        turn(p)
    wz_leaf = {}
    for p in FIRST:
        wz_first[p].wait_recv()
        at = z_at(-p)
        for d, way in children(p, 0):
            wz_leaf[d] = send(wz.at[at], wz.at[at], device(0, 0, way, 0))
    settle()
    for d in LEAVES[::-1]:
        for h in range(2):
            leaf_out[d, h].wait_recv()
        turn(d)

    back_copy = []
    for dy in (2, 1, -1, 0):
        if dy == 0:
            for d in LEAVES:
                wz_leaf[d].wait_recv()
            grad = wz[0].astype(F32)
            for k in range(1, NZ):
                grad = grad + wz[k].astype(F32)
            wt[block(i, 16), :] = grad.astype(BF16)
            wt_copy = [
                send(wt.at[block(i, 16)], wt.at[block(i, 16)], device(dx, dy, 0, 0)) for dx, dy in XY
            ]
        group = lax.rem(y + (dy + NY), NY)
        value = jnp.dot(slope_t[...], dense[:, block(group, NX * B)], preferred_element_type=F32)
        for k in range(NX):
            back_s[group * NX + k] = value[:, k * B : (k + 1) * B].astype(BF16)
            if dy == 0:
                spread_t[k] = value[:, k * B : (k + 1) * B]
        for dx in (2, 1, -1, 0):
            if (dx, dy) != (0, 0):
                k = XY.index((dx, dy))
                back_copy.append(send(back_s.at[row_at(dx, dy)], back_r.at[k], device(dx, dy, 0, 0)))

    for copy in back_copy:
        copy.wait_recv()
    total = spread_t[x]
    for k in range(len(XY)):
        total = total + back_r[k].astype(F32)
    fg_out[...] = total.T.astype(BF16)

    for copy in wt_copy:
        copy.wait_recv()
    wg_out[...] = wt[...].astype(F32)
    settle()


def hand_on(*refs):
    n = len(refs) // 2
    for k in range(n):
        refs[n + k][...] = refs[k][...]


def per_device(features, weight, tiles, tile_blocks, tile_counts, cotangent):
    vmem = pl.BlockSpec(memory_space=pltpu.VMEM)
    hbm = pl.BlockSpec(memory_space=pl.ANY)
    n_xy = len(XY)
    scratch = [
        pltpu.VMEM((B + 1, B, B), BF16),
        pltpu.VMEM((NODES, NODES), BF16),
        pltpu.VMEM((NODES, B), BF16),
        pltpu.VMEM((2, B), jnp.int32),
        pltpu.VMEM((8, B), jnp.int32),
        pltpu.SMEM((8, B), jnp.int32),
        pltpu.VMEM((2, 2 * B, B), BF16),
        pltpu.VMEM((B, B), BF16),
        pltpu.VMEM((2, HB, B), BF16),
        pltpu.VMEM((len(LEAVES), B, B), BF16),
        pltpu.VMEM((len(LEAVES), B, B), BF16),
        pltpu.VMEM((len(FIRST) + 1, B, B), F32),
        pltpu.VMEM((len(FIRST), B, B), BF16),
        pltpu.VMEM((len(FIRST), 2, HB, B), BF16),
        pltpu.VMEM((HB, B), BF16),
        pltpu.VMEM((HB, B), BF16),
        pltpu.VMEM((2, HB, B), F32),
        pltpu.VMEM((2, HB, B), BF16),
        pltpu.VMEM((HB, B), BF16),
        pltpu.VMEM((2, HB, B), BF16),
        pltpu.VMEM((NODES, B), BF16),
        pltpu.VMEM((B, NODES), BF16),
        pltpu.VMEM((NX, B, B), F32),
        pltpu.VMEM((BPP, B, B), BF16),
        pltpu.VMEM((n_xy, B, B), BF16),
        pltpu.VMEM((2, 2 * B, B), F32),
        pltpu.VMEM((2 * B, B), BF16),
        pltpu.VMEM((2 * B, B), BF16),
        pltpu.VMEM((2 * B, B), F32),
        pltpu.VMEM((2 * B, B), BF16),
        pltpu.VMEM((n_xy, 16, B), BF16),
        pltpu.VMEM((NZ, 16, B), BF16),
        pltpu.VMEM((2 * B, B), BF16),
        pltpu.SemaphoreType.DMA((8,)),
        pltpu.SemaphoreType.DMA,
        pltpu.SemaphoreType.DMA((N_SEMS,)),
        pltpu.SemaphoreType.DMA((N_SEMS,)),
    ]
    out_shape = (
        jax.ShapeDtypeStruct((B, B), BF16),
        jax.ShapeDtypeStruct((B, B), BF16),
        jax.ShapeDtypeStruct((2 * B, B), F32),
    )
    results = pl.pallas_call(
        kernel,
        out_shape=(pltpu.VMEM((B, B), BF16), pltpu.VMEM((B, B), BF16), pltpu.VMEM((2 * B, B), F32)),
        in_specs=[hbm, hbm, hbm, hbm, vmem, hbm],
        out_specs=(vmem, vmem, vmem),
        scratch_shapes=scratch,
        compiler_params=pltpu.CompilerParams(collective_id=0, has_side_effects=True, vmem_limit_bytes=56 * 2**20),
        cost_estimate=pl.CostEstimate(flops=4 * NODES * NODES * B, bytes_accessed=2**23, transcendentals=B * B),
        name="gcn",
    )(features, weight, cotangent, tile_blocks, tile_counts, tiles)
    results = pl.pallas_call(
        hand_on,
        out_shape=out_shape,
        in_specs=[vmem] * 3,
        out_specs=(vmem, vmem, vmem),
        cost_estimate=pl.CostEstimate(flops=0, bytes_accessed=2**19, transcendentals=0),
        name="hand_on",
    )(*[pltpu.with_memory_space_constraint(r, pltpu.VMEM) for r in results])
    return tuple(results)


def solution(mesh):
    return jax.shard_map(
        per_device,
        mesh=mesh,
        in_specs=(
            P(("col", "row"), None),
            P(None, "dep"),
            P("row", "col", None, None, None),
            P("row", "col", None, None),
            P("row", "col"),
            P(("row", "col"), "dep"),
        ),
        out_specs=(P(("row", "col"), "dep"), P(("col", "row"), "dep"), P(None, "dep")),
        check_vma=False,
    )
```

```python
import functools

import jax
import jax.numpy as jnp
from jax import lax
from jax.experimental import pallas as pl
from jax.experimental.pallas import tpu as pltpu
from jax.sharding import PartitionSpec as P

MESH = pl.DeviceIdType.MESH
F32, BF16 = jnp.float32, jnp.bfloat16
B = 128
BPP = 16
NODES = BPP * B
HB = B // 2
NX, NY, NZ = 4, 4, 16
XY = sorted(
    [(dx, dy) for dx in (0, 1, -1, 2) for dy in (0, 1, -1, 2) if (dx, dy) != (0, 0)],
    key=lambda o: (-(abs(o[0]) + abs(o[1])), (o[0] + 2 * o[1]) % 5),
)
TREE = {5: (7, 6, 4), 2: (3,), 1: ()}
FAR = max(TREE)
CHILDREN = {s * p: tuple(s * d for d in ds) for p, ds in TREE.items() for s in (1, -1)}
FIRST = tuple(CHILDREN)
INNER = tuple(p for p in FIRST if CHILDREN[p] or abs(p) == FAR)
NEAR = tuple(p for p in FIRST if p not in INNER)
PARENT = {d: p for p, ds in CHILDREN.items() for d in ds}
LEAVES = (8,) + tuple(sorted(PARENT, key=lambda d: (-abs(d), -d)))


def children(p, h):
    pairs = [(d, d - p) for d in CHILDREN[p]]
    if p == FAR and h == 0:
        pairs = [(8, 8 - FAR)] + pairs
    if p == -FAR and h == 1:
        pairs = [(8, FAR - 8)] + pairs
    return pairs


def way_up(d, h):
    if d == 8:
        return FAR - 8 if h == 0 else 8 - FAR
    return PARENT[d] - d


PEERS = sorted(
    [(dx, dy, 0, 0) for dx, dy in XY]
    + [(0, 0, d, 0) for d in sorted({w for p in FIRST for h in range(2) for _, w in children(p, h)} | set(FIRST))]
    + [(0, 0, d, 1) for d in FIRST]
    + [(0, 0, 0, 1)],
    key=lambda o: -sum(map(abs, o)),
)
N_SEMS = 160


def kernel(
    feat, weight, cot, blocks, counts, tiles, act_out, fg_out, wg_out,
    tile_v, dense, gath, blk_v, inv_v, inv_s, w_all, cot_v, cot_h, leaf_s, leaf_r, part, first_s, first_r,
    sib_s, sib_r, agg, act_s, act_r, slope_s, slope_p, slope_t, spread_t, back_s, back_r, wgp, wg_s, wg_r, wg_t, wc_s,
    wc_r, wz, wt, load_sem, inv_sem, send_sem, recv_sem,
):
    i = lax.axis_index("row")
    z = lax.axis_index("col")
    c = lax.axis_index("dep")
    x, y = lax.rem(i, NX), lax.div(i, NX)

    def row_at(dx, dy):
        return lax.rem(y + (dy + NY), NY) * NX + lax.rem(x + (dx + NX), NX)

    def z_at(d):
        return lax.rem(z + (d + NZ), NZ)

    def device(dx, dy, dz, dc):
        return (row_at(dx, dy), z_at(dz), 1 - c if dc else c)

    def block(at, size=B):
        return pl.ds(pl.multiple_of(at * size, size), size)

    def piece(at, h):
        return pl.ds(pl.multiple_of(at * B + h * HB, HB), HB)

    counter = [0]
    sent = []

    def slots(n):
        counter[0] += n
        return counter[0] - n

    def remote(src, dst, where, send_k, recv_k):
        return pltpu.make_async_remote_copy(
            src_ref=src, dst_ref=dst, send_sem=send_sem.at[send_k], recv_sem=recv_sem.at[recv_k],
            device_id=where, device_id_type=MESH,
        )

    def send(src, dst, where):
        k = slots(1)
        copy = remote(src, dst, where, k, k)
        copy.start()
        sent.append(copy)
        return copy

    def settle():
        for copy in sent:
            copy.wait_send()
        sent.clear()

    def send_to_core(src, dst, z_to, q, k):
        copy = remote(src, dst, (i, z_to, jnp.int32(q)), k + q, k + c)
        copy.start()
        sent.append(copy)

    def expect(dst, k):
        return remote(dst, dst, (i, z, 1 - c), k, k)

    barrier = pltpu.get_barrier_semaphore()
    for peer in PEERS:
        pl.semaphore_signal(barrier, inc=1, device_id=device(*peer), device_id_type=MESH)
    loads = []

    def load(src, dst):
        copy = pltpu.make_async_copy(src, dst, load_sem.at[len(loads)])
        copy.start()
        loads.append(copy)
        return copy

    own = block(i)
    got_blocks = load(blocks.at[0, 0], blk_v)
    got_feat = load(feat.at[:, block(c)], gath.at[own])
    own_w = load(weight, w_all.at[c])
    own_cot = load(cot, cot_v)
    got_tiles = [load(tiles.at[0, 0, pl.ds(q * 32, 32)], tile_v.at[pl.ds(q * 32, 32)]) for q in range(4)]

    got_blocks.wait()
    flat = blk_v[0:1, :] * BPP + blk_v[1:2, :]
    lane = lax.broadcasted_iota(jnp.int32, (1, B), 1)
    flat = jnp.where(lane < jnp.broadcast_to(counts[...], (1, B)), flat, -1)
    flat = jnp.broadcast_to(flat, (B, B)).T
    slot = lax.broadcasted_iota(jnp.int32, (B, B), 0) - B
    place = lax.broadcasted_iota(jnp.int32, (B, B), 1)
    inv_v[...] = jnp.zeros_like(inv_v)
    for h in range(2):
        hit = jnp.where(flat == place + h * B, slot, 0)
        inv_v[h : h + 1, :] = jnp.clip(jnp.sum(hit, axis=0, keepdims=True) + B, 0, B)
    inv_copy = pltpu.make_async_copy(inv_v, inv_s, inv_sem)
    inv_copy.start()
    tile_v[B] = jnp.zeros((B, B), BF16)
    got_feat.wait()
    own_w.wait()
    own_cot.wait()
    cot_h[c] = cot_v[block(c, HB), :]

    pl.semaphore_wait(barrier, len(PEERS))

    gathered = [send(gath.at[own], gath.at[own], device(dx, dy, 0, 0)) for dx, dy in XY]
    got_w = send(w_all.at[c], w_all.at[c], device(0, 0, 0, 1))
    got_cot = send(cot_v.at[block(1 - c, HB)], cot_h.at[c], device(0, 0, 0, 1))

    inv_copy.wait()
    for copy in got_tiles:
        copy.wait()

    @pl.loop(0, BPP)
    def _(r):
        rows = block(r)
        for col in range(BPP):
            at = r * BPP + col
            dense[rows, col * B : (col + 1) * B] = tile_v[inv_s[lax.div(at, B), lax.rem(at, B)]]

    for copy in gathered:
        copy.wait_recv()

    def chunk(d):
        return jnp.dot(dense[block(z_at(-d)), :], gath[...], preferred_element_type=F32)

    halves_of = [pl.ds(h * HB, HB) for h in range(2)]
    leaf_copy = {}

    def send_leaf(d, h):
        k = LEAVES.index(d)
        leaf_copy[d, h] = send(
            leaf_s.at[k, halves_of[h]], leaf_r.at[k, halves_of[h]], device(0, 0, way_up(d, h), 0)
        )

    for k, d in enumerate(LEAVES):
        leaf_s[k] = chunk(d).astype(BF16)
        for h in range(2):
            send_leaf(d, h)
    for k, p in enumerate(FIRST):
        value = chunk(p)
        if p in INNER:
            part[k] = value
        else:
            first_s[k] = value.astype(BF16)
    part[len(FIRST)] = chunk(0)
    first_k = {p: slots(2) for p in FIRST}

    def send_first(p, h):
        k = FIRST.index(p)
        if p in INNER:
            total = part[k, halves_of[h], :]
            for d, _ in children(p, h):
                leaf_copy[d, h].wait_recv()
                total = total + leaf_r[LEAVES.index(d), halves_of[h], :].astype(F32)
            first_s[k, halves_of[h], :] = total.astype(BF16)
        send_to_core(first_s.at[k, halves_of[h]], first_r.at[k, c], z_at(-p), h, first_k[p])

    sib_s[...] = part[len(FIRST), block(1 - c, HB), :].astype(BF16)
    sib_copy = send(sib_s, sib_r, device(0, 0, 0, 1))
    agg[c] = part[len(FIRST), block(c, HB), :]
    for h in range(2):
        for p in NEAR + INNER:
            send_first(p, h)
    early = sent[:-12]
    for copy in early:
        copy.wait_send()
    del sent[:-12]
    sib_copy.wait_recv()
    agg[1 - c] = sib_r[...].astype(F32)
    got_w.wait_recv()
    got_cot.wait_recv()
    for p in FIRST:
        for q in range(2):
            expect(first_r.at[FIRST.index(p), q], first_k[p] + q).wait_recv()
    halves = []
    for h in range(2):
        total = agg[h]
        for k in range(len(FIRST)):
            total = total + first_r[k, h].astype(F32)
        halves.append(total.astype(BF16))

    slopes = []
    for u in range(2):
        pre = sum(
            jnp.dot(halves[h], w_all[u, h * B : (h + 1) * B, :], preferred_element_type=F32) for h in range(2)
        )
        squash = jnp.tanh(pre)
        act_s[u] = squash.astype(BF16)
        slopes.append((cot_h[u].astype(F32) * (1.0 - squash * squash)).astype(BF16))
    for h in range(2):
        back = sum(
            lax.dot_general(
                slopes[u], w_all[u, h * B : (h + 1) * B, :], (((1,), (1,)), ((), ())), preferred_element_type=F32
            )
            for u in range(2)
        )
        slope_s[h] = back.astype(BF16)

    here = piece(z, c)
    out_k = {p: slots(2) for p in FIRST}
    for p in FIRST:
        for q in range(2):
            send_to_core(slope_s.at[q], slope_p.at[here], z_at(p), q, out_k[p])
    near = send(slope_s.at[1 - c], slope_p.at[here], device(0, 0, 0, 1))
    slope_p[here, :] = slope_s[c]

    for u in range(2):
        for h in range(2):
            wgp[u, h * B : (h + 1) * B, :] = lax.dot_general(
                halves[h], slopes[u], (((0,), (0,)), ((), ())), preferred_element_type=F32
            )
    wg_s[...] = wgp[1 - c].astype(BF16)
    wg_copy = send(wg_s, wg_r, device(0, 0, 0, 1))
    act_copy = send(act_s.at[1 - c], act_r, device(0, 0, 0, 1))
    act_out[block(c, HB), :] = act_s[c]

    leaf_out = {}

    def forward(p, h):
        rows = piece(z_at(-p), h)
        expect(slope_p.at[rows], out_k[p] + h).wait_recv()
        for d, way in children(p, h):
            leaf_out[d, h] = send(slope_p.at[rows], slope_p.at[rows], device(0, 0, way, 0))

    wg_copy.wait_recv()
    wg_t[...] = wgp[c] + wg_r[...].astype(F32)
    wc_s[...] = wg_t[...].astype(BF16)
    wc_copy = [
        send(wc_s.at[block(row_at(dx, dy), 16)], wc_r.at[k], device(dx, dy, 0, 0))
        for k, (dx, dy) in enumerate(XY)
    ]
    early = sent[:-15]
    for copy in early:
        copy.wait_send()
    del sent[:-15]
    for p in INNER:
        forward(p, 0)
    for copy in wc_copy:
        copy.wait_recv()
    total = wg_t[block(i, 16), :]
    for k in range(len(XY)):
        total = total + wc_r[k].astype(F32)
    wz[z] = total.astype(BF16)
    wz_first = {p: send(wz.at[z], wz.at[z], device(0, 0, p, 0)) for p in FIRST}

    for p in INNER:
        forward(p, 1)

    act_copy.wait_recv()
    act_out[block(1 - c, HB), :] = act_r[...]

    def turn(d):
        slope_t[:, block(z_at(-d))] = slope_p[block(z_at(-d)), :].T

    near.wait_recv()
    turn(0)
    for p in NEAR:
        for q in range(2):
            expect(slope_p.at[piece(z_at(-p), q)], out_k[p] + q).wait_recv()
        turn(p)
    for p in INNER:
        turn(p)
    wz_leaf = {}
    for p in FIRST:
        wz_first[p].wait_recv()
        at = z_at(-p)
        for d, way in children(p, 0):
            wz_leaf[d] = send(wz.at[at], wz.at[at], device(0, 0, way, 0))
    settle()
    for d in LEAVES[::-1]:
        for h in range(2):
            leaf_out[d, h].wait_recv()
        turn(d)

    back_copy = []
    for dy in (2, 1, -1, 0):
        if dy == 0:
            for d in LEAVES:
                wz_leaf[d].wait_recv()
            grad = wz[0].astype(F32)
            for k in range(1, NZ):
                grad = grad + wz[k].astype(F32)
            wt[block(i, 16), :] = grad.astype(BF16)
            wt_copy = [
                send(wt.at[block(i, 16)], wt.at[block(i, 16)], device(dx, dy, 0, 0)) for dx, dy in XY
            ]
        group = lax.rem(y + (dy + NY), NY)
        value = jnp.dot(slope_t[...], dense[:, block(group, NX * B)], preferred_element_type=F32)
        for k in range(NX):
            back_s[group * NX + k] = value[:, k * B : (k + 1) * B].astype(BF16)
            if dy == 0:
                spread_t[k] = value[:, k * B : (k + 1) * B]
        for dx in (2, 1, -1, 0):
            if (dx, dy) != (0, 0):
                k = XY.index((dx, dy))
                back_copy.append(send(back_s.at[row_at(dx, dy)], back_r.at[k], device(dx, dy, 0, 0)))

    for copy in back_copy:
        copy.wait_recv()
    total = spread_t[x]
    for k in range(len(XY)):
        total = total + back_r[k].astype(F32)
    fg_out[...] = total.T.astype(BF16)

    for copy in wt_copy:
        copy.wait_recv()
    wg_out[...] = wt[...].astype(F32)
    settle()


def hand_on(*refs):
    n = len(refs) // 2
    for k in range(n):
        refs[n + k][...] = refs[k][...]


def per_device(features, weight, tiles, tile_blocks, tile_counts, cotangent):
    vmem = pl.BlockSpec(memory_space=pltpu.VMEM)
    hbm = pl.BlockSpec(memory_space=pl.ANY)
    n_xy = len(XY)
    scratch = [
        pltpu.VMEM((B + 1, B, B), BF16),
        pltpu.VMEM((NODES, NODES), BF16),
        pltpu.VMEM((NODES, B), BF16),
        pltpu.VMEM((2, B), jnp.int32),
        pltpu.VMEM((8, B), jnp.int32),
        pltpu.SMEM((8, B), jnp.int32),
        pltpu.VMEM((2, 2 * B, B), BF16),
        pltpu.VMEM((B, B), BF16),
        pltpu.VMEM((2, HB, B), BF16),
        pltpu.VMEM((len(LEAVES), B, B), BF16),
        pltpu.VMEM((len(LEAVES), B, B), BF16),
        pltpu.VMEM((len(FIRST) + 1, B, B), F32),
        pltpu.VMEM((len(FIRST), B, B), BF16),
        pltpu.VMEM((len(FIRST), 2, HB, B), BF16),
        pltpu.VMEM((HB, B), BF16),
        pltpu.VMEM((HB, B), BF16),
        pltpu.VMEM((2, HB, B), F32),
        pltpu.VMEM((2, HB, B), BF16),
        pltpu.VMEM((HB, B), BF16),
        pltpu.VMEM((2, HB, B), BF16),
        pltpu.VMEM((NODES, B), BF16),
        pltpu.VMEM((B, NODES), BF16),
        pltpu.VMEM((NX, B, B), F32),
        pltpu.VMEM((BPP, B, B), BF16),
        pltpu.VMEM((n_xy, B, B), BF16),
        pltpu.VMEM((2, 2 * B, B), F32),
        pltpu.VMEM((2 * B, B), BF16),
        pltpu.VMEM((2 * B, B), BF16),
        pltpu.VMEM((2 * B, B), F32),
        pltpu.VMEM((2 * B, B), BF16),
        pltpu.VMEM((n_xy, 16, B), BF16),
        pltpu.VMEM((NZ, 16, B), BF16),
        pltpu.VMEM((2 * B, B), BF16),
        pltpu.SemaphoreType.DMA((8,)),
        pltpu.SemaphoreType.DMA,
        pltpu.SemaphoreType.DMA((N_SEMS,)),
        pltpu.SemaphoreType.DMA((N_SEMS,)),
    ]
    out_shape = (
        jax.ShapeDtypeStruct((B, B), BF16),
        jax.ShapeDtypeStruct((B, B), BF16),
        jax.ShapeDtypeStruct((2 * B, B), F32),
    )
    results = pl.pallas_call(
        kernel,
        out_shape=(pltpu.VMEM((B, B), BF16), pltpu.VMEM((B, B), BF16), pltpu.VMEM((2 * B, B), F32)),
        in_specs=[hbm, hbm, hbm, hbm, vmem, hbm],
        out_specs=(vmem, vmem, vmem),
        scratch_shapes=scratch,
        compiler_params=pltpu.CompilerParams(collective_id=0, has_side_effects=True, vmem_limit_bytes=56 * 2**20),
        cost_estimate=pl.CostEstimate(flops=4 * NODES * NODES * B, bytes_accessed=2**23, transcendentals=B * B),
        name="gcn",
    )(features, weight, cotangent, tile_blocks, tile_counts, tiles)
    results = pl.pallas_call(
        hand_on,
        out_shape=out_shape,
        in_specs=[vmem] * 3,
        out_specs=(vmem, vmem, vmem),
        cost_estimate=pl.CostEstimate(flops=0, bytes_accessed=2**19, transcendentals=0),
        name="hand_on",
    )(*[pltpu.with_memory_space_constraint(r, pltpu.VMEM) for r in results])
    return tuple(results)


def solution(mesh):
    return jax.shard_map(
        per_device,
        mesh=mesh,
        in_specs=(
            P(("col", "row"), None),
            P(None, "dep"),
            P("row", "col", None, None, None),
            P("row", "col", None, None),
            P("row", "col"),
            P(("row", "col"), "dep"),
        ),
        out_specs=(P(("row", "col"), "dep"), P(("col", "row"), "dep"), P(None, "dep")),
        check_vma=False,
    )
```
